32 devices in a mesh: grains: 32 (over z, y, x, core).
Axes of the slice: x: 2, y: 2, z: 4, core: 2. Of those that a mesh axis runs over, the one named last changes fastest.
Arguments:
- tangent: float32 [2048, 128, 128], P('grains'), may hold values from -48 to 48
- blocks: bfloat16 [2048, 8, 128, 128], P('grains'), may hold values from -0.1875 to 0.1875
- columns: int32 [2048, 8], P('grains'), may hold values from 0 to 95, as said below
- counts: int32 [32], P('grains'), may hold values from 32 to 64, as said below
- send_lists: int32 [32, 2, 16], P('grains'), may hold values from 0 to 63, as said below
Outputs:
- basis: float32 [2048, 128, 128], P('grains')
- r_factor: float32 [128, 128], replicated
The draws below stay inside these ranges and needn't reach their ends.
Inputs may be any that keep to these rules, and one draw needn't show every extreme that they name: `counts`: some device has exactly 64 live block rows; every device has at least 32. Every entry of send_lists[d] is below counts[d]. For block row b of device d, columns[., 0] is b; every other entry is below counts[d] or lies in 64 to 64 + 2 * 16 - 1 (received rows). Entries of slots that are not live follow the same law.
All inputs are finite; a program needn't handle non-finite values.
Results may differ from the reference program's by a relative error of at most 0.0028.
Values may be sent and summed in bfloat16 or wider, within the bound.
A program may use at most 128 MiB of HBM per device.

```python
import jax
import jax.numpy as jnp
from jax import lax

BR = 64
B = 128
K = 128
NNZ = 8
H = 16
SUBSTEPS = 3
ROWS = 2048
N_GRAINS = 32


def shared_layout(key):
    base = jax.random.fold_in(key, 7)
    sizes = jax.random.randint(jax.random.fold_in(base, 1), (N_GRAINS,), BR // 2, BR + 1)
    chosen = jax.random.randint(jax.random.fold_in(base, 2), (), 0, N_GRAINS)
    device_ids = jnp.arange(N_GRAINS, dtype=jnp.int32)
    sizes = jnp.where(device_ids == chosen, BR, sizes).astype(jnp.int32)
    sends = jax.random.randint(jax.random.fold_in(base, 3), (N_GRAINS, 2, H), 0, sizes[:, None, None])
    sends = sends.at[chosen, 0, 0].set(BR - 1)
    sends = sends.at[chosen, 1, 0].set(0)
    raw = jax.random.randint(jax.random.fold_in(base, 4), (N_GRAINS, BR, NNZ), 0, sizes[:, None, None] + 2 * H)
    mapped = jnp.where(raw < sizes[:, None, None], raw, raw - sizes[:, None, None] + BR)
    own = jnp.broadcast_to(jnp.arange(BR, dtype=jnp.int32)[None, :], (N_GRAINS, BR))
    mapped = mapped.at[:, :, 0].set(own)
    mapped = mapped.at[chosen, 0, 1].set(BR + 2 * H - 1)
    return (sizes, sends.astype(jnp.int32), mapped.reshape(N_GRAINS * BR, NNZ).astype(jnp.int32))


def draw_counts(key, part):
    return shared_layout(key)[0]


def draw_send_lists(key, part):
    return shared_layout(key)[1]


def draw_columns(key, part):
    return shared_layout(key)[2]


def draw_tangent(key, part):
    position = jnp.arange(N_GRAINS * BR, dtype=jnp.float32) // BR / max(N_GRAINS - 1, 1)
    noise = jnp.clip(jax.random.normal(jax.random.fold_in(key, 11), (N_GRAINS * BR, B, K), jnp.float32), -6.0, 6.0)
    scales = jnp.exp(jnp.log(4.0) * position)
    return (noise * scales[:, None, None]).astype(jnp.float32)


def levels(rng, dims, split, least, largest):
    gain, own = 1.0, jax.random.fold_in(rng, 6)
    for dim, parts in split:
        heights = jnp.exp(jax.random.uniform(jax.random.fold_in(own, dim), (parts,), jnp.float32, least / len(split), largest / len(split)))
        gain = gain * jnp.repeat(heights, dims[dim] // parts).reshape([-1 if axis == dim else 1 for axis in range(len(dims))])
    return gain


def gaussian(own_key, extent, deviation, limit, shards=(), held_as=jnp.bfloat16):
    drawn = jax.random.normal(own_key, extent, jnp.float32) * deviation
    if len(shards) > 0:
        drawn = levels(own_key, extent, shards, -0.22, 0.18) * drawn
    return jnp.clip(drawn, min=-limit, max=limit).astype(held_as)


def setup_inputs(seed: int = 0) -> dict:
    streams_of = jax.random.split(jax.random.key(seed), 6)
    tangent = draw_tangent(jax.random.fold_in(streams_of[5], 71), 0)
    blocks = gaussian(streams_of[1], (ROWS, NNZ, B, B), (B * NNZ) ** -0.5, 0.1875, ((0, 32),))
    columns = draw_columns(jax.random.fold_in(streams_of[5], 71), 0)
    counts = draw_counts(jax.random.fold_in(streams_of[5], 71), 0)
    send_lists = draw_send_lists(jax.random.fold_in(streams_of[5], 71), 0)
    return {"tangent": tangent, "blocks": blocks, "columns": columns, "counts": counts, "send_lists": send_lists}


def pick_rows(rounded, indices):
    return rounded[indices]

def propagate(args):
    extended, cols, blk = args
    gathered = extended[cols]
    return jnp.einsum('bkij,bkjv->biv', blk.astype(jnp.float32), gathered.astype(jnp.float32), precision=lax.Precision.HIGHEST)

def reference(tangent, blocks, columns, counts, send_lists):
    live = (jnp.arange(BR, dtype=jnp.int32)[None, :] < counts[:, None]).astype(jnp.float32)
    mask = live.reshape(N_GRAINS * BR, 1, 1)
    state = tangent * mask
    cols = columns.reshape(N_GRAINS, BR, NNZ)
    blk = blocks.reshape(N_GRAINS, BR, NNZ, B, B)
    for step in range(SUBSTEPS):
        rounded = state.astype(jnp.bfloat16).reshape(N_GRAINS, BR, B, K)
        to_lower = jax.vmap(pick_rows)(rounded, send_lists[:, 0])
        to_upper = jax.vmap(pick_rows)(rounded, send_lists[:, 1])
        from_lower = jnp.roll(to_upper, 1, axis=0)
        from_upper = jnp.roll(to_lower, -1, axis=0)
        extended = jnp.concatenate([rounded, from_lower, from_upper], axis=1)
        update = lax.map(propagate, (extended, cols, blk)).reshape(N_GRAINS * BR, B, K)
        state = state + update * mask
    flat = state.reshape(N_GRAINS * BR * B, K)
    q_full, r_full = jnp.linalg.qr(flat)
    signs = jnp.sign(jnp.diagonal(r_full))
    basis = (q_full * signs[None, :]).reshape(N_GRAINS * BR, B, K)
    return (basis, r_full * signs[:, None])
```

```python
import functools

import jax
import jax.numpy as jnp
from jax import lax
from jax.experimental import pallas as pl
from jax.experimental.pallas import tpu as pltpu
from jax.sharding import PartitionSpec as P

SUBSTEPS = 3
GROUP = 8
CHUNKS = 8
MESH = pl.DeviceIdType.MESH
F32 = jnp.float32
BF16 = jnp.bfloat16


def split(x):
    hi = x.astype(BF16)
    lo = (x - hi.astype(F32)).astype(BF16)
    return hi, lo


def propagate_kernel(n, columns, counts, lists, tangent, blocks, state_out, gram_out,
                     state, ext0, ext1, outgoing, landing, held, gram, parts, across,
                     load_sem, blk_sem, out_sem, halo_send, halo_recv,
                     rs_send, rs_recv, ac_send, ac_recv, ag_send, ag_recv):
    me = lax.axis_index("grains")
    lower, upper = lax.rem(me + n - 1, n), lax.rem(me + 1, n)
    slots, nnz, width, _ = blocks.shape
    sent = lists.shape[2]
    group, rank = me // GROUP, lax.rem(me, GROUP)
    n_groups = n // GROUP
    rows = width // GROUP
    exts = (ext0, ext1)
    step_rows = slots // CHUNKS

    load = pltpu.make_async_copy(tangent, state, load_sem)
    load.start()
    for c in range(CHUNKS):
        part = pl.ds(c * step_rows, step_rows)
        pltpu.make_async_copy(blocks.at[part], held.at[part], blk_sem.at[c]).start()

    mates = [group * GROUP + lax.rem(rank + off, GROUP) for off in range(1, GROUP)]
    others = [lax.rem(group + off, n_groups) * GROUP + rank for off in range(1, n_groups)]
    barrier = pltpu.get_barrier_semaphore()
    peers = [lower, upper] + mates + others
    for peer in peers:
        pl.semaphore_signal(barrier, inc=1, device_id=(peer,), device_id_type=MESH)

    live_count = counts[0]

    def alive(b):
        return jnp.where(b < live_count, 1.0, 0.0).astype(F32)

    load.wait()

    @pl.loop(0, slots)
    def _(b):
        value = state[b] * alive(b)
        state[b] = value
        ext0[b] = value.astype(BF16)

    pl.semaphore_wait(barrier, len(peers))

    for step in range(SUBSTEPS):
        ext, later = exts[step % 2], exts[(step + 1) % 2]
        sends = []
        for way, peer in ((1, upper), (0, lower)):
            @pl.loop(0, sent)
            def _(i):
                outgoing[step % 2, way, i] = ext[lists[0, way, i]]

            copy = pltpu.make_async_remote_copy(
                src_ref=outgoing.at[step % 2, way],
                dst_ref=landing.at[step, way],
                send_sem=halo_send.at[step, way],
                recv_sem=halo_recv.at[step, way],
                device_id=(peer,),
                device_id_type=MESH,
            )
            copy.start()
            sends.append(copy)
        if step == 0:
            for c in range(CHUNKS):
                part = pl.ds(c * step_rows, step_rows)
                pltpu.make_async_copy(blocks.at[part], held.at[part], blk_sem.at[c]).wait()
        for copy in sends:
            copy.wait()

        @pl.loop(0, sent)
        def _(i):
            ext[slots + i] = landing[step, 1, i]
            ext[slots + sent + i] = landing[step, 0, i]

        @pl.loop(0, slots)
        def _(b):
            left = jnp.concatenate([held[b, k] for k in range(nnz)], axis=1)
            right = jnp.concatenate([ext[columns[b, k]] for k in range(nnz)], axis=0)
            update = jnp.dot(left, right, preferred_element_type=F32)
            value = state[b] + update * alive(b)
            state[b] = value
            if step < SUBSTEPS - 1:
                later[b] = value.astype(BF16)

    store = pltpu.make_async_copy(state, state_out, out_sem)
    store.start()

    per = 4

    def add(i, total):
        hi, lo = split(state[pl.ds(i * per, per)].reshape(per * width, width))
        both = jnp.concatenate([hi, lo], axis=1)
        return total + lax.dot_general(hi, both, (((0,), (0,)), ((), ())), preferred_element_type=F32)

    total = lax.fori_loop(0, slots // per, add, jnp.zeros((width, 2 * width), F32))
    cross = total[:, width:]
    gram[...] = total[:, :width] + cross + cross.T

    def mine(r):
        return pl.ds(pl.multiple_of(r * rows, rows), rows)

    copies = []
    for off in range(1, GROUP):
        copy = pltpu.make_async_remote_copy(
            src_ref=gram.at[mine(lax.rem(rank + off, GROUP))],
            dst_ref=parts.at[off - 1],
            send_sem=rs_send.at[off - 1],
            recv_sem=rs_recv.at[off - 1],
            device_id=(mates[off - 1],),
            device_id_type=MESH,
        )
        copy.start()
        copies.append(copy)
    value = gram[mine(rank)]
    for off, copy in enumerate(copies):
        copy.wait_recv()
        value = value + parts[off]
    across[group] = value
    for copy in copies:
        copy.wait_send()
    copies = []
    for off in range(1, n_groups):
        copy = pltpu.make_async_remote_copy(
            src_ref=across.at[group],
            dst_ref=across.at[group],
            send_sem=ac_send.at[off - 1],
            recv_sem=ac_recv.at[off - 1],
            device_id=(others[off - 1],),
            device_id_type=MESH,
        )
        copy.start()
        copies.append(copy)
    for copy in copies:
        copy.wait()
    value = across[0]
    for g in range(1, n_groups):
        value = value + across[g]
    gram_out[mine(rank)] = value
    copies = []
    for off in range(1, GROUP):
        copy = pltpu.make_async_remote_copy(
            src_ref=gram_out.at[mine(rank)],
            dst_ref=gram_out.at[mine(rank)],
            send_sem=ag_send.at[off - 1],
            recv_sem=ag_recv.at[off - 1],
            device_id=(mates[off - 1],),
            device_id_type=MESH,
        )
        copy.start()
        copies.append(copy)
    for copy in copies:
        copy.wait()
    store.wait()


def factor_kernel(gram, flat, basis, r_factor, weights):
    size = gram.shape[0]
    sub = 8

    @pl.when(pl.program_id(0) == 0)
    def _():
        g = gram[...]
        row = lax.broadcasted_iota(jnp.int32, (size, size), 0)
        col = lax.broadcasted_iota(jnp.int32, (size, size), 1)
        eye = jnp.where(row == col, 1.0, 0.0).astype(F32)
        both = jnp.concatenate([g, eye], axis=1)
        line = lax.broadcasted_iota(jnp.int32, (sub, 1), 0)
        done = []
        for p in range(size // sub):
            panel = both[:sub]
            for c in range(sub):
                j = p * sub + c
                root = lax.rsqrt(panel[c:c + 1, j:j + 1])
                unit = panel[c:c + 1] * root
                scale = jnp.where(line > c, panel[:, j:j + 1] * root, 0.0)
                panel = jnp.where(line == c, unit, panel - scale * unit)
            done.append(panel)
            if p < size // sub - 1:
                fall = lax.dot_general(panel[:, :size], panel, (((0,), (0,)), ((), ())),
                                       precision=lax.Precision.HIGHEST, preferred_element_type=F32)
                both = both[sub:] - fall[(p + 1) * sub:]
        full = jnp.concatenate(done, axis=0)
        r_factor[...] = jnp.where(row <= col, full[:, :size], 0.0)
        inverse = full[:, size:].T
        hi, lo = split(inverse)
        pair = jnp.concatenate([hi, lo], axis=1)
        weights[...] = jnp.concatenate([pair, pair], axis=0)

    hi, lo = split(flat[...])
    left = jnp.concatenate([hi, lo], axis=1)
    out = jnp.dot(left, weights[...], preferred_element_type=F32)
    basis[...] = out[:, :size] + out[:, size:]


def local(n, tangent, blocks, columns, counts, send_lists):
    slots, width, vectors = tangent.shape
    nnz = blocks.shape[1]
    sent = send_lists.shape[2]
    n_groups = n // GROUP
    rows = width // GROUP
    smem = pl.BlockSpec(memory_space=pltpu.SMEM)
    hbm = pl.BlockSpec(memory_space=pl.ANY)
    dma = pltpu.SemaphoreType.DMA
    extended = (slots + 2 * sent, width, vectors)
    state, gram = pl.pallas_call(
        functools.partial(propagate_kernel, n),
        out_shape=(
            jax.ShapeDtypeStruct((slots, width, vectors), F32),
            jax.ShapeDtypeStruct((vectors, vectors), F32),
        ),
        in_specs=[smem, smem, smem, hbm, hbm],
        out_specs=(hbm, pl.BlockSpec(memory_space=pltpu.VMEM)),
        scratch_shapes=[
            pltpu.VMEM((slots, width, vectors), F32),
            pltpu.VMEM(extended, BF16),
            pltpu.VMEM(extended, BF16),
            pltpu.VMEM((2, 2, sent, width, vectors), BF16),
            pltpu.VMEM((SUBSTEPS, 2, sent, width, vectors), BF16),
            pltpu.VMEM((slots, nnz, width, width), BF16),
            pltpu.VMEM((vectors, vectors), F32),
            pltpu.VMEM((GROUP - 1, rows, vectors), F32),
            pltpu.VMEM((n_groups, rows, vectors), F32),
            dma, dma((CHUNKS,)), dma,
            dma((SUBSTEPS, 2)), dma((SUBSTEPS, 2)),
            dma((GROUP - 1,)), dma((GROUP - 1,)),
            dma((max(n_groups - 1, 1),)), dma((max(n_groups - 1, 1),)),
            dma((GROUP - 1,)), dma((GROUP - 1,)),
        ],
        compiler_params=pltpu.CompilerParams(
            collective_id=0, has_side_effects=True, vmem_limit_bytes=48 * 2**20),
        name="propagate",
    )(columns, counts, send_lists, tangent, blocks)

    tall = slots * width
    tiles = 8
    basis, r_factor = pl.pallas_call(
        factor_kernel,
        grid=(tiles,),
        out_shape=(
            jax.ShapeDtypeStruct((tall, vectors), F32),
            jax.ShapeDtypeStruct((vectors, vectors), F32),
        ),
        in_specs=[
            pl.BlockSpec((vectors, vectors), lambda i: (0, 0)),
            pl.BlockSpec((tall // tiles, vectors), lambda i: (i, 0)),
        ],
        out_specs=(
            pl.BlockSpec((tall // tiles, vectors), lambda i: (i, 0)),
            pl.BlockSpec((vectors, vectors), lambda i: (0, 0)),
        ),
        scratch_shapes=[pltpu.VMEM((2 * vectors, 2 * vectors), BF16)],
        compiler_params=pltpu.CompilerParams(vmem_limit_bytes=32 * 2**20),
        name="factor",
    )(gram, state.reshape(tall, vectors))
    return basis.reshape(slots, width, vectors), r_factor


def solution(mesh):
    in_specs = (
        P("grains", None, None),
        P("grains", None, None, None),
        P("grains", None),
        P("grains"),
        P("grains", None, None),
    )
    out_specs = (P("grains", None, None), P())
    n = mesh.shape["grains"]
    return jax.shard_map(functools.partial(local, n), mesh=mesh, in_specs=in_specs, out_specs=out_specs, check_vma=False)
```

```python
import functools

import jax
import jax.numpy as jnp
from jax import lax
from jax.experimental import pallas as pl
from jax.experimental.pallas import tpu as pltpu
from jax.sharding import PartitionSpec as P

SUBSTEPS = 3
GROUP = 8
CHUNKS = 8
PIECES = 2
MESH = pl.DeviceIdType.MESH
F32 = jnp.float32
BF16 = jnp.bfloat16


def split(x):
    hi = x.astype(BF16)
    lo = (x - hi.astype(F32)).astype(BF16)
    return hi, lo


def propagate_kernel(n, columns, counts, lists, tangent, blocks, state_out, gram_out,
                     state, ext0, ext1, outgoing, landing, held, gram, parts, across,
                     load_sem, blk_sem, out_sem, halo_send, halo_recv,
                     rs_send, rs_recv, ac_send, ac_recv, ag_send, ag_recv):
    me = lax.axis_index("grains")
    lower, upper = lax.rem(me + n - 1, n), lax.rem(me + 1, n)
    slots, nnz, width, _ = blocks.shape
    sent = lists.shape[2]
    group, rank = me // GROUP, lax.rem(me, GROUP)
    n_groups = n // GROUP
    rows = width // GROUP
    exts = (ext0, ext1)
    step_rows = slots // CHUNKS

    load = pltpu.make_async_copy(tangent, state, load_sem)
    load.start()
    for c in range(CHUNKS):
        part = pl.ds(c * step_rows, step_rows)
        pltpu.make_async_copy(blocks.at[part], held.at[part], blk_sem.at[c]).start()

    mates = [group * GROUP + lax.rem(rank + off, GROUP) for off in range(1, GROUP)]
    others = [lax.rem(group + off, n_groups) * GROUP + rank for off in range(1, n_groups)]
    barrier = pltpu.get_barrier_semaphore()
    peers = [lower, upper] + mates + others
    for peer in peers:
        pl.semaphore_signal(barrier, inc=1, device_id=(peer,), device_id_type=MESH)

    live_count = counts[0]

    def alive(b):
        return jnp.where(b < live_count, 1.0, 0.0).astype(F32)

    load.wait()

    @pl.loop(0, slots, unroll=4)
    def _(b):
        value = state[b] * alive(b)
        state[b] = value
        ext0[b] = value.astype(BF16)

    pl.semaphore_wait(barrier, len(peers))

    half = sent // PIECES

    def send(step, way, piece):
        part = pl.ds(piece * half, half)
        copy = pltpu.make_async_remote_copy(
            src_ref=outgoing.at[step % 2, way, part],
            dst_ref=landing.at[step, way, part],
            send_sem=halo_send.at[step, way, piece],
            recv_sem=halo_recv.at[step, way, piece],
            device_id=(upper if way == 1 else lower,),
            device_id_type=MESH,
        )
        copy.start()
        return copy

    def advanced(ext, b):
        left = jnp.concatenate([held[b, k] for k in range(nnz)], axis=1)
        right = jnp.concatenate([ext[columns[b, k]] for k in range(nnz)], axis=0)
        update = jnp.dot(left, right, preferred_element_type=F32)
        return state[b] + update * alive(b)

    order = [(way, piece) for piece in range(PIECES) for way in (1, 0)]
    sends = []
    for way, piece in order:
        @pl.loop(piece * half, (piece + 1) * half, unroll=4)
        def _(i):
            outgoing[0, way, i] = ext0[lists[0, way, i]]

        sends.append(send(0, way, piece))
    for c in range(CHUNKS):
        part = pl.ds(c * step_rows, step_rows)
        pltpu.make_async_copy(blocks.at[part], held.at[part], blk_sem.at[c]).wait()

    for step in range(SUBSTEPS):
        ext, later = exts[step % 2], exts[(step + 1) % 2]
        for copy in sends:
            copy.wait()

        @pl.loop(0, sent, unroll=4)
        def _(i):
            ext[slots + i] = landing[step, 1, i]
            ext[slots + sent + i] = landing[step, 0, i]

        sends = []
        if step < SUBSTEPS - 1:
            for way, piece in order:
                @pl.loop(piece * half, (piece + 1) * half, unroll=8)
                def _(i):
                    outgoing[(step + 1) % 2, way, i] = advanced(ext, lists[0, way, i]).astype(BF16)

                sends.append(send(step + 1, way, piece))

        @pl.loop(0, slots, unroll=8)
        def _(b):
            value = advanced(ext, b)
            state[b] = value
            if step < SUBSTEPS - 1:
                later[b] = value.astype(BF16)

    store = pltpu.make_async_copy(state, state_out, out_sem)
    store.start()

    per = 4

    def add(i, total):
        hi, lo = split(state[pl.ds(i * per, per)].reshape(per * width, width))
        both = jnp.concatenate([hi, lo], axis=1)
        return total + lax.dot_general(hi, both, (((0,), (0,)), ((), ())), preferred_element_type=F32)

    total = lax.fori_loop(0, slots // per, add, jnp.zeros((width, 2 * width), F32))
    cross = total[:, width:]
    gram[...] = total[:, :width] + cross + cross.T

    def mine(r):
        return pl.ds(pl.multiple_of(r * rows, rows), rows)

    copies = []
    for off in range(1, GROUP):
        copy = pltpu.make_async_remote_copy(
            src_ref=gram.at[mine(lax.rem(rank + off, GROUP))],
            dst_ref=parts.at[off - 1],
            send_sem=rs_send.at[off - 1],
            recv_sem=rs_recv.at[off - 1],
            device_id=(mates[off - 1],),
            device_id_type=MESH,
        )
        copy.start()
        copies.append(copy)
    value = gram[mine(rank)]
    for off, copy in enumerate(copies):
        copy.wait_recv()
        value = value + parts[off]
    across[group] = value
    for copy in copies:
        copy.wait_send()
    copies = []
    for off in range(1, n_groups):
        copy = pltpu.make_async_remote_copy(
            src_ref=across.at[group],
            dst_ref=across.at[group],
            send_sem=ac_send.at[off - 1],
            recv_sem=ac_recv.at[off - 1],
            device_id=(others[off - 1],),
            device_id_type=MESH,
        )
        copy.start()
        copies.append(copy)
    for copy in copies:
        copy.wait()
    value = across[0]
    for g in range(1, n_groups):
        value = value + across[g]
    gram_out[mine(rank)] = value
    copies = []
    for off in range(1, GROUP):
        copy = pltpu.make_async_remote_copy(
            src_ref=gram_out.at[mine(rank)],
            dst_ref=gram_out.at[mine(rank)],
            send_sem=ag_send.at[off - 1],
            recv_sem=ag_recv.at[off - 1],
            device_id=(mates[off - 1],),
            device_id_type=MESH,
        )
        copy.start()
        copies.append(copy)
    for copy in copies:
        copy.wait()
    store.wait()


def thirds(x):
    hi = x.astype(BF16).astype(F32)
    rest = x - hi
    mid = rest.astype(BF16).astype(F32)
    return hi, mid, rest - mid


def factor_kernel(gram, flat, basis, r_factor, weights, held, load_sem):
    size = gram.shape[0]
    sub = 8
    tile = basis.shape[0]
    load = pltpu.make_async_copy(flat, held, load_sem)

    @pl.when(pl.program_id(0) == 0)
    def _():
        load.start()
        row = lax.broadcasted_iota(jnp.int32, (size, size), 0)
        col = lax.broadcasted_iota(jnp.int32, (size, size), 1)
        left = gram[...]
        right = jnp.where(row == col, 1.0, 0.0).astype(F32)
        line = lax.broadcasted_iota(jnp.int32, (sub, size), 0)
        factors, inverses = [], []
        for p in range(size // sub):
            a, e = left[:sub], right[:sub]
            spread = [jnp.broadcast_to(a[:, j:j + 1], (sub, size)) for j in range(p * sub, (p + 1) * sub)]
            for c in range(sub):
                root = lax.rsqrt(spread[c][c:c + 1])
                scale = jnp.where(line > c, spread[c] * root, 0.0)
                for d in range(c + 1, sub):
                    spread[d] = spread[d] - scale * (spread[d][c:c + 1] * root)
                unit = a[c:c + 1] * root
                a = jnp.where(line == c, unit, a - scale * unit)
                unit = e[c:c + 1] * root
                e = jnp.where(line == c, unit, e - scale * unit)
            factors.append(a)
            inverses.append(e)
            if p < size // sub - 1:
                hi, mid, lo = thirds(a)
                ehi, emid, elo = thirds(e)
                lhs = jnp.concatenate([hi, hi, hi, mid, mid, lo], axis=0).astype(BF16)
                rhs = jnp.concatenate([
                    jnp.concatenate([hi, mid, lo, hi, mid, hi], axis=0),
                    jnp.concatenate([ehi, emid, elo, ehi, emid, ehi], axis=0)], axis=1).astype(BF16)
                fall = lax.dot_general(lhs, rhs, (((0,), (0,)), ((), ())), preferred_element_type=F32)
                left = left[sub:] - fall[(p + 1) * sub:, :size]
                right = right[sub:] - fall[(p + 1) * sub:, size:]
        r_factor[...] = jnp.where(row <= col, jnp.concatenate(factors, axis=0), 0.0)
        inverse = jnp.concatenate(inverses, axis=0).T
        hi, lo = split(inverse)
        pair = jnp.concatenate([hi, lo], axis=1)
        weights[...] = jnp.concatenate([pair, pair], axis=0)
        load.wait()

    here = pl.ds(pl.multiple_of(pl.program_id(0) * tile, tile), tile)
    hi, lo = split(held[here])
    both = jnp.concatenate([hi, lo], axis=1)
    out = jnp.dot(both, weights[...], preferred_element_type=F32)
    basis[...] = out[:, :size] + out[:, size:]


def local(n, tangent, blocks, columns, counts, send_lists):
    slots, width, vectors = tangent.shape
    nnz = blocks.shape[1]
    sent = send_lists.shape[2]
    n_groups = n // GROUP
    rows = width // GROUP
    smem = pl.BlockSpec(memory_space=pltpu.SMEM)
    hbm = pl.BlockSpec(memory_space=pl.ANY)
    dma = pltpu.SemaphoreType.DMA
    extended = (slots + 2 * sent, width, vectors)
    state, gram = pl.pallas_call(
        functools.partial(propagate_kernel, n),
        out_shape=(
            jax.ShapeDtypeStruct((slots, width, vectors), F32),
            jax.ShapeDtypeStruct((vectors, vectors), F32),
        ),
        in_specs=[smem, smem, smem, hbm, hbm],
        out_specs=(hbm, pl.BlockSpec(memory_space=pltpu.VMEM)),
        scratch_shapes=[
            pltpu.VMEM((slots, width, vectors), F32),
            pltpu.VMEM(extended, BF16),
            pltpu.VMEM(extended, BF16),
            pltpu.VMEM((2, 2, sent, width, vectors), BF16),
            pltpu.VMEM((SUBSTEPS, 2, sent, width, vectors), BF16),
            pltpu.VMEM((slots, nnz, width, width), BF16),
            pltpu.VMEM((vectors, vectors), F32),
            pltpu.VMEM((GROUP - 1, rows, vectors), F32),
            pltpu.VMEM((n_groups, rows, vectors), F32),
            dma, dma((CHUNKS,)), dma,
            dma((SUBSTEPS, 2, PIECES)), dma((SUBSTEPS, 2, PIECES)),
            dma((GROUP - 1,)), dma((GROUP - 1,)),
            dma((max(n_groups - 1, 1),)), dma((max(n_groups - 1, 1),)),
            dma((GROUP - 1,)), dma((GROUP - 1,)),
        ],
        compiler_params=pltpu.CompilerParams(
            collective_id=0, has_side_effects=True, vmem_limit_bytes=48 * 2**20),
        name="propagate",
    )(columns, counts, send_lists, tangent, blocks)

    tall = slots * width
    tiles = 8
    basis, r_factor = pl.pallas_call(
        factor_kernel,
        grid=(tiles,),
        out_shape=(
            jax.ShapeDtypeStruct((tall, vectors), F32),
            jax.ShapeDtypeStruct((vectors, vectors), F32),
        ),
        in_specs=[
            pl.BlockSpec((vectors, vectors), lambda i: (0, 0)),
            hbm,
        ],
        out_specs=(
            pl.BlockSpec((tall // tiles, vectors), lambda i: (i, 0)),
            pl.BlockSpec((vectors, vectors), lambda i: (0, 0)),
        ),
        scratch_shapes=[pltpu.VMEM((2 * vectors, 2 * vectors), BF16), pltpu.VMEM((tall, vectors), F32), dma],
        compiler_params=pltpu.CompilerParams(vmem_limit_bytes=32 * 2**20),
        name="factor",
    )(gram, state.reshape(tall, vectors))
    return basis.reshape(slots, width, vectors), r_factor


def solution(mesh):
    in_specs = (
        P("grains", None, None),
        P("grains", None, None, None),
        P("grains", None),
        P("grains"),
        P("grains", None, None),
    )
    out_specs = (P("grains", None, None), P())
    n = mesh.shape["grains"]
    return jax.shard_map(functools.partial(local, n), mesh=mesh, in_specs=in_specs, out_specs=out_specs, check_vma=False)
```

```python
import functools

import jax
import jax.numpy as jnp
from jax import lax
from jax.experimental import pallas as pl
from jax.experimental.pallas import tpu as pltpu
from jax.sharding import PartitionSpec as P

SUBSTEPS = 3
GROUP = 8
CHUNKS = 8
PIECES = 2
MESH = pl.DeviceIdType.MESH
F32 = jnp.float32
BF16 = jnp.bfloat16


def split(x):
    hi = x.astype(BF16)
    lo = (x - hi.astype(F32)).astype(BF16)
    return hi, lo


def propagate_kernel(n, columns, counts, lists, tangent, blocks, state_out, gram_out,
                     state, ext0, ext1, outgoing, landing, held, gram, parts, across,
                     load_sem, blk_sem, out_sem, halo_send, halo_recv,
                     rs_send, rs_recv, ac_send, ac_recv, ag_send, ag_recv):
    me = lax.axis_index("grains")
    lower, upper = lax.rem(me + n - 1, n), lax.rem(me + 1, n)
    slots, nnz, width, _ = blocks.shape
    sent = lists.shape[2]
    group, rank = me // GROUP, lax.rem(me, GROUP)
    n_groups = n // GROUP
    rows = width // GROUP
    exts = (ext0, ext1)
    step_rows = slots // CHUNKS

    load = pltpu.make_async_copy(tangent, state, load_sem)
    load.start()
    for c in range(CHUNKS):
        part = pl.ds(c * step_rows, step_rows)
        pltpu.make_async_copy(blocks.at[part], held.at[part], blk_sem.at[c]).start()

    mates = [group * GROUP + lax.rem(rank + off, GROUP) for off in range(1, GROUP)]
    others = [lax.rem(group + off, n_groups) * GROUP + rank for off in range(1, n_groups)]
    barrier = pltpu.get_barrier_semaphore()
    peers = [lower, upper] + mates + others
    for peer in peers:
        pl.semaphore_signal(barrier, inc=1, device_id=(peer,), device_id_type=MESH)

    live_count = counts[0]

    def alive(b):
        return jnp.where(b < live_count, 1.0, 0.0).astype(F32)

    load.wait()

    @pl.loop(0, slots, unroll=4)
    def _(b):
        value = state[b] * alive(b)
        state[b] = value
        ext0[b] = value.astype(BF16)

    pl.semaphore_wait(barrier, len(peers))

    half = sent // PIECES

    def send(step, way, piece):
        part = pl.ds(piece * half, half)
        copy = pltpu.make_async_remote_copy(
            src_ref=outgoing.at[step % 2, way, part],
            dst_ref=landing.at[step, way, part],
            send_sem=halo_send.at[step, way, piece],
            recv_sem=halo_recv.at[step, way, piece],
            device_id=(upper if way == 1 else lower,),
            device_id_type=MESH,
        )
        copy.start()
        return copy

    def advanced(ext, b):
        left = jnp.concatenate([held[b, k] for k in range(nnz)], axis=1)
        right = jnp.concatenate([ext[columns[b, k]] for k in range(nnz)], axis=0)
        update = jnp.dot(left, right, preferred_element_type=F32)
        return state[b] + update * alive(b)

    order = [(way, piece) for piece in range(PIECES) for way in (1, 0)]
    sends = []
    for way, piece in order:
        @pl.loop(piece * half, (piece + 1) * half, unroll=4)
        def _(i):
            outgoing[0, way, i] = ext0[lists[0, way, i]]

        sends.append(send(0, way, piece))
    for c in range(CHUNKS):
        part = pl.ds(c * step_rows, step_rows)
        pltpu.make_async_copy(blocks.at[part], held.at[part], blk_sem.at[c]).wait()

    for step in range(SUBSTEPS):
        ext, later = exts[step % 2], exts[(step + 1) % 2]
        for copy in sends:
            copy.wait()

        @pl.loop(0, sent, unroll=4)
        def _(i):
            ext[slots + i] = landing[step, 1, i]
            ext[slots + sent + i] = landing[step, 0, i]

        sends = []
        if step < SUBSTEPS - 1:
            for way, piece in order:
                @pl.loop(piece * half, (piece + 1) * half, unroll=8)
                def _(i):
                    outgoing[(step + 1) % 2, way, i] = advanced(ext, lists[0, way, i]).astype(BF16)

                sends.append(send(step + 1, way, piece))

        if step < SUBSTEPS - 1:
            @pl.loop(0, slots, unroll=8)
            def _(b):
                value = advanced(ext, b)
                state[b] = value
                later[b] = value.astype(BF16)

    per = 8

    def finish(i, total):
        values = [advanced(ext, i * per + t) for t in range(per)]
        for t in range(per):
            state[i * per + t] = values[t]
        hi, lo = split(jnp.concatenate(values, axis=0))
        both = jnp.concatenate([hi, lo], axis=1)
        return total + lax.dot_general(hi, both, (((0,), (0,)), ((), ())), preferred_element_type=F32)

    total = lax.fori_loop(0, slots // per, finish, jnp.zeros((width, 2 * width), F32))
    store = pltpu.make_async_copy(state, state_out, out_sem)
    store.start()
    cross = total[:, width:]
    gram[...] = total[:, :width] + cross + cross.T

    def mine(r):
        return pl.ds(pl.multiple_of(r * rows, rows), rows)

    copies = []
    for off in range(1, GROUP):
        copy = pltpu.make_async_remote_copy(
            src_ref=gram.at[mine(lax.rem(rank + off, GROUP))],
            dst_ref=parts.at[off - 1],
            send_sem=rs_send.at[off - 1],
            recv_sem=rs_recv.at[off - 1],
            device_id=(mates[off - 1],),
            device_id_type=MESH,
        )
        copy.start()
        copies.append(copy)
    value = gram[mine(rank)]
    for off, copy in enumerate(copies):
        copy.wait_recv()
        value = value + parts[off]
    across[group] = value
    for copy in copies:
        copy.wait_send()
    copies = []
    for off in range(1, n_groups):
        copy = pltpu.make_async_remote_copy(
            src_ref=across.at[group],
            dst_ref=across.at[group],
            send_sem=ac_send.at[off - 1],
            recv_sem=ac_recv.at[off - 1],
            device_id=(others[off - 1],),
            device_id_type=MESH,
        )
        copy.start()
        copies.append(copy)
    for copy in copies:
        copy.wait()
    value = across[0]
    for g in range(1, n_groups):
        value = value + across[g]
    gram_out[mine(rank)] = value
    copies = []
    for off in range(1, GROUP):
        copy = pltpu.make_async_remote_copy(
            src_ref=gram_out.at[mine(rank)],
            dst_ref=gram_out.at[mine(rank)],
            send_sem=ag_send.at[off - 1],
            recv_sem=ag_recv.at[off - 1],
            device_id=(mates[off - 1],),
            device_id_type=MESH,
        )
        copy.start()
        copies.append(copy)
    for copy in copies:
        copy.wait()
    store.wait()


def thirds(x):
    hi = x.astype(BF16).astype(F32)
    rest = x - hi
    mid = rest.astype(BF16).astype(F32)
    return hi, mid, rest - mid


def factor_kernel(gram, flat, basis, r_factor, weights, held, load_sem):
    size = gram.shape[0]
    sub = 8
    tile = basis.shape[0]
    load = pltpu.make_async_copy(flat, held, load_sem)

    @pl.when(pl.program_id(0) == 0)
    def _():
        load.start()
        row = lax.broadcasted_iota(jnp.int32, (size, size), 0)
        col = lax.broadcasted_iota(jnp.int32, (size, size), 1)
        left = gram[...]
        right = jnp.where(row == col, 1.0, 0.0).astype(F32)
        line = lax.broadcasted_iota(jnp.int32, (sub, size), 0)
        factors, inverses = [], []
        for p in range(size // sub):
            a, e = left[:sub], right[:sub]
            spread = [jnp.broadcast_to(a[:, j:j + 1], (sub, size)) for j in range(p * sub, (p + 1) * sub)]
            for c in range(sub):
                root = lax.rsqrt(spread[c][c:c + 1])
                scale = jnp.where(line > c, spread[c] * root, 0.0)
                for d in range(c + 1, sub):
                    spread[d] = spread[d] - scale * (spread[d][c:c + 1] * root)
                unit = a[c:c + 1] * root
                a = jnp.where(line == c, unit, a - scale * unit)
                unit = e[c:c + 1] * root
                e = jnp.where(line == c, unit, e - scale * unit)
            factors.append(a)
            inverses.append(e)
            if p < size // sub - 1:
                hi, mid, lo = thirds(a)
                ehi, emid, elo = thirds(e)
                lhs = jnp.concatenate([hi, hi, hi, mid, mid, lo], axis=0).astype(BF16)
                rhs = jnp.concatenate([
                    jnp.concatenate([hi, mid, lo, hi, mid, hi], axis=0),
                    jnp.concatenate([ehi, emid, elo, ehi, emid, ehi], axis=0)], axis=1).astype(BF16)
                fall = lax.dot_general(lhs, rhs, (((0,), (0,)), ((), ())), preferred_element_type=F32)
                left = left[sub:] - fall[(p + 1) * sub:, :size]
                right = right[sub:] - fall[(p + 1) * sub:, size:]
        r_factor[...] = jnp.where(row <= col, jnp.concatenate(factors, axis=0), 0.0)
        inverse = jnp.concatenate(inverses, axis=0).T
        hi, lo = split(inverse)
        pair = jnp.concatenate([hi, lo], axis=1)
        weights[...] = jnp.concatenate([pair, pair], axis=0)
        load.wait()

    here = pl.ds(pl.multiple_of(pl.program_id(0) * tile, tile), tile)
    hi, lo = split(held[here])
    both = jnp.concatenate([hi, lo], axis=1)
    out = jnp.dot(both, weights[...], preferred_element_type=F32)
    basis[...] = out[:, :size] + out[:, size:]


def local(n, tangent, blocks, columns, counts, send_lists):
    slots, width, vectors = tangent.shape
    nnz = blocks.shape[1]
    sent = send_lists.shape[2]
    n_groups = n // GROUP
    rows = width // GROUP
    smem = pl.BlockSpec(memory_space=pltpu.SMEM)
    hbm = pl.BlockSpec(memory_space=pl.ANY)
    dma = pltpu.SemaphoreType.DMA
    extended = (slots + 2 * sent, width, vectors)
    state, gram = pl.pallas_call(
        functools.partial(propagate_kernel, n),
        out_shape=(
            jax.ShapeDtypeStruct((slots, width, vectors), F32),
            jax.ShapeDtypeStruct((vectors, vectors), F32),
        ),
        in_specs=[smem, smem, smem, hbm, hbm],
        out_specs=(hbm, pl.BlockSpec(memory_space=pltpu.VMEM)),
        scratch_shapes=[
            pltpu.VMEM((slots, width, vectors), F32),
            pltpu.VMEM(extended, BF16),
            pltpu.VMEM(extended, BF16),
            pltpu.VMEM((2, 2, sent, width, vectors), BF16),
            pltpu.VMEM((SUBSTEPS, 2, sent, width, vectors), BF16),
            pltpu.VMEM((slots, nnz, width, width), BF16),
            pltpu.VMEM((vectors, vectors), F32),
            pltpu.VMEM((GROUP - 1, rows, vectors), F32),
            pltpu.VMEM((n_groups, rows, vectors), F32),
            dma, dma((CHUNKS,)), dma,
            dma((SUBSTEPS, 2, PIECES)), dma((SUBSTEPS, 2, PIECES)),
            dma((GROUP - 1,)), dma((GROUP - 1,)),
            dma((max(n_groups - 1, 1),)), dma((max(n_groups - 1, 1),)),
            dma((GROUP - 1,)), dma((GROUP - 1,)),
        ],
        compiler_params=pltpu.CompilerParams(
            collective_id=0, has_side_effects=True, vmem_limit_bytes=48 * 2**20),
        name="propagate",
    )(columns, counts, send_lists, tangent, blocks)

    tall = slots * width
    tiles = 8
    basis, r_factor = pl.pallas_call(
        factor_kernel,
        grid=(tiles,),
        out_shape=(
            jax.ShapeDtypeStruct((tall, vectors), F32),
            jax.ShapeDtypeStruct((vectors, vectors), F32),
        ),
        in_specs=[
            pl.BlockSpec((vectors, vectors), lambda i: (0, 0)),
            hbm,
        ],
        out_specs=(
            pl.BlockSpec((tall // tiles, vectors), lambda i: (i, 0)),
            pl.BlockSpec((vectors, vectors), lambda i: (0, 0)),
        ),
        scratch_shapes=[pltpu.VMEM((2 * vectors, 2 * vectors), BF16), pltpu.VMEM((tall, vectors), F32), dma],
        compiler_params=pltpu.CompilerParams(vmem_limit_bytes=32 * 2**20),
        name="factor",
    )(gram, state.reshape(tall, vectors))
    return basis.reshape(slots, width, vectors), r_factor


def solution(mesh):
    in_specs = (
        P("grains", None, None),
        P("grains", None, None, None),
        P("grains", None),
        P("grains"),
        P("grains", None, None),
    )
    out_specs = (P("grains", None, None), P())
    n = mesh.shape["grains"]
    return jax.shard_map(functools.partial(local, n), mesh=mesh, in_specs=in_specs, out_specs=out_specs, check_vma=False)
```
